512 devices in a mesh: ctx: 32 (over z, x), exp: 16 (over y, core).
Axes of the slice: x: 4, y: 8, z: 8, core: 2. Of those that a mesh axis runs over, the one named last changes fastest.
Arguments:
- x_ssd: bfloat16 [65536, 4096], P('ctx', 'exp'), may hold values from -6 to 6
- dt_raw: float32 [65536, 64], P('ctx', 'exp'), may hold values from -9 to -3
- a_log: float32 [64], P('exp')
- b_in: bfloat16 [65536, 1024], P('ctx', 'exp'), may hold values from -6 to 6
- c_in: bfloat16 [65536, 1024], P('ctx', 'exp'), may hold values from -0.5390625 to 0.5390625
- d_skip: float32 [64], P('exp'), may hold values from 0.1 to 2.5
- dy_ssd: bfloat16 [65536, 4096], P('ctx', 'exp'), may hold values from -6 to 6
Outputs:
- input_gradient: bfloat16 [65536, 4096], P('ctx', 'exp')
- grad_dt: float32 [65536, 64], P('ctx', 'exp')
- sensitivity_loga: float32 [64], P('exp')
- grad_b: bfloat16 [65536, 1024], P('ctx', 'exp')
- grad_c: bfloat16 [65536, 1024], P('ctx', 'exp')
- grad_dskip: float32 [64], P('exp')
The draws below stay inside these ranges and needn't reach their ends.
All inputs are finite; a program needn't handle non-finite values.
Results may differ from the reference program's by a relative error of at most 0.00105.
Values may be sent and summed in bfloat16 or wider, within the bound.
No kernel may reach another device: no remote copies, remote signals or barrier semaphores. Data moves between devices by JAX's collectives and lax.ppermute only.
A program may use at most 128 MiB of HBM per device.

```python
import jax
import jax.numpy as jnp
from jax import lax

CHANNEL_WIDTH = 64
STATE = 128
BLOCK = 128
HEADS = 64
GROUPS = 8
STREAM_LENGTH = 65536


def draw_dt_raw(key, part):
    key_noise = jax.random.fold_in(key, 11)
    position = jnp.arange(STREAM_LENGTH, dtype=jnp.float32)
    drift = 0.5 * jnp.sin(6.283185307 * 3.0 * position / STREAM_LENGTH)
    noise = jnp.clip(0.5 * jax.random.normal(key_noise, (STREAM_LENGTH, HEADS), jnp.float32), -1.5, 1.5)
    return (-6.0 + drift[:, None] + noise).astype(jnp.float32)


def draw_a_log(key, part):
    key_pick = jax.random.fold_in(key, 21)
    key_fast = jax.random.fold_in(key, 22)
    key_slow = jax.random.fold_in(key, 23)
    is_fast = jax.random.randint(key_pick, (HEADS,), 0, 10) < 5
    fast_rate = jax.random.uniform(key_fast, (HEADS,), jnp.float32, 10.0, 16.0)
    slow_rate = jax.random.uniform(key_slow, (HEADS,), jnp.float32, 0.2, 0.6) * 400.0 / STREAM_LENGTH
    return jnp.log(jnp.where(is_fast, fast_rate, slow_rate)).astype(jnp.float32)


def block_scale(own_key, extent, cuts, least, largest):
    def one(dim, shards_of):
        heights = jax.random.uniform(jax.random.fold_in(jax.random.fold_in(own_key, 6), dim), (shards_of,), jnp.float32, least / len(cuts), largest / len(cuts))
        return jnp.repeat(jnp.exp(heights), extent[dim] // shards_of).reshape((-1,) + (1,) * (len(extent) - dim - 1))

    loudness = one(*cuts[0])
    for cut in cuts[1:]:
        loudness = loudness * one(*cut)
    return loudness


def scatter_about(key, shape, deviation, bound, split=(), held_as=jnp.bfloat16):
    array = deviation * jax.random.normal(key, shape, jnp.float32)
    if split:
        array = array * block_scale(key, shape, split, -0.22, 0.18)
    return jnp.clip(array, -bound, bound).astype(held_as)


def setup_inputs(seed: int = 0) -> dict:
    streams_of = jax.random.split(jax.random.key(seed), 8)
    return {
        "x_ssd": scatter_about(streams_of[0], (STREAM_LENGTH, HEADS * CHANNEL_WIDTH), 1.0, 6.0, ((0, 32), (1, 16))),
        "dt_raw": draw_dt_raw(jax.random.fold_in(streams_of[7], 71), 0),
        "a_log": draw_a_log(jax.random.fold_in(streams_of[7], 71), 0),
        "b_in": scatter_about(streams_of[3], (STREAM_LENGTH, GROUPS * STATE), 1.0, 6.0, ((0, 32), (1, 16))),
        "c_in": scatter_about(streams_of[4], (STREAM_LENGTH, GROUPS * STATE), 0.09, 0.5390625, ((0, 32), (1, 16))),
        "d_skip": jnp.clip(0.1 + 2.4 * jax.random.uniform(streams_of[5], (HEADS,), jnp.float32) ** block_scale(streams_of[5], (HEADS,), ((0, 16),), -0.2, 0.2), 0.1, 2.5),
        "dy_ssd": scatter_about(streams_of[6], (STREAM_LENGTH, HEADS * CHANNEL_WIDTH), 1.0, 6.0, ((0, 32), (1, 16))),
    }


precise = lax.Precision.HIGHEST

def ssd_forward(values_in, dt_values, log_decay, b_values, c_values, skip_weight, start_state, block_len):
    length, head_count = dt_values.shape
    groups = b_values.shape[1]
    head_width = values_in.shape[1] // head_count
    values = values_in.reshape(length, head_count, head_width)
    step_size = jax.nn.softplus(dt_values)
    log_rate = -jnp.exp(log_decay)[None, :] * step_size
    b_heads = jnp.repeat(b_values, head_count // groups, axis=1)
    c_heads = jnp.repeat(c_values, head_count // groups, axis=1)
    blocks = length // block_len
    lower_mask = (jnp.arange(block_len)[:, None] >= jnp.arange(block_len)[None, :])[:, :, None]

    def blocked(array_in):
        return array_in.reshape((blocks, block_len) + array_in.shape[1:])

    def advance(carry_state, pieces):
        block_values, block_steps, block_rates, block_b, block_c = pieces
        cumulative = jnp.cumsum(block_rates, axis=0)
        spread = jnp.where(lower_mask, cumulative[:, None, :] - cumulative[None, :, :], 0.0)
        decay_lookup = jnp.where(lower_mask, jnp.exp(spread), 0.0)
        scores = jnp.einsum('thn,shn->tsh', block_c, block_b, precision=precise)
        inputs = block_steps[:, :, None] * block_values
        inner_part = jnp.einsum('tsh,shp->thp', decay_lookup * scores, inputs, precision=precise)
        carried = jnp.exp(cumulative)[:, :, None] * jnp.einsum('thn,hpn->thp', block_c, carry_state, precision=precise)
        block_out = inner_part + carried + skip_weight[None, :, None] * block_values
        tail_decay = jnp.exp(cumulative[-1][None, :] - cumulative)
        following = jnp.exp(cumulative[-1])[:, None, None] * carry_state + jnp.einsum('sh,shp,shn->hpn', tail_decay, inputs, block_b, precision=precise)
        return (following, block_out)
    final_state, outputs = lax.scan(jax.checkpoint(advance), start_state, (blocked(values), blocked(step_size), blocked(log_rate), blocked(b_heads), blocked(c_heads)))
    return (outputs.reshape(length, head_count * head_width), final_state)

def reference(x_ssd, dt_raw, a_log, b_in, c_in, d_skip, dy_ssd):
    per_group = HEADS // GROUPS

    def divided_heads(array_in, width):
        return jnp.transpose(array_in.reshape(STREAM_LENGTH, GROUPS, per_group * width), (1, 0, 2))

    def split_state(array_in):
        return jnp.transpose(array_in.astype(jnp.float32).reshape(STREAM_LENGTH, GROUPS, 1, STATE), (1, 0, 2, 3))
    values_g = divided_heads(x_ssd.astype(jnp.float32), CHANNEL_WIDTH)
    upstream_g = divided_heads(dy_ssd.astype(jnp.float32), CHANNEL_WIDTH)
    steps_g = divided_heads(dt_raw, 1)
    logs_g = a_log.reshape(GROUPS, per_group)
    skips_g = d_skip.reshape(GROUPS, per_group)
    b_g = split_state(b_in)
    c_g = split_state(c_in)
    start_state = jnp.zeros((per_group, CHANNEL_WIDTH, STATE), jnp.float32)

    def one_group(pieces):
        values_in, steps_in, logs_in, b_full, c_full, skips, upstream = pieces

        def forward(values_a, steps_a, logs_a, b_a, c_a, skips_a):
            return ssd_forward(values_a, steps_a, logs_a, b_a, c_a, skips_a, start_state, BLOCK)[0]
        _, pullback = jax.vjp(forward, values_in, steps_in, logs_in, b_full, c_full, skips)
        return pullback(upstream)
    grad_vals, grad_dt, sensitivity_loga, grad_bvals, grad_cvals, grad_dskip = lax.map(one_group, (values_g, steps_g, logs_g, b_g, c_g, skips_g, upstream_g))
    input_gradient = jnp.transpose(grad_vals, (1, 0, 2)).reshape(STREAM_LENGTH, HEADS * CHANNEL_WIDTH).astype(jnp.bfloat16)
    grad_dt = jnp.transpose(grad_dt, (1, 0, 2)).reshape(STREAM_LENGTH, HEADS)
    grad_b = jnp.transpose(grad_bvals, (1, 0, 2, 3)).reshape(STREAM_LENGTH, GROUPS * STATE).astype(jnp.bfloat16)
    grad_c = jnp.transpose(grad_cvals, (1, 0, 2, 3)).reshape(STREAM_LENGTH, GROUPS * STATE).astype(jnp.bfloat16)
    return (input_gradient, grad_dt, sensitivity_loga.reshape(HEADS), grad_b, grad_c, grad_dskip.reshape(HEADS))
```

```python
import functools

import jax
import jax.numpy as jnp
from jax import lax
from jax.experimental import pallas as pl
from jax.experimental.pallas import tpu as pltpu
from jax.sharding import PartitionSpec as P

T = 128
F32 = jnp.float32
BF16 = jnp.bfloat16
VMEM_LIMIT = 56 * 2**20
TURNS = 2


def dot(a, b, contract=((1,), (0,)), precision=None):
    return lax.dot_general(a, b, (contract, ((), ())), precision=precision, preferred_element_type=F32)


NT = ((1,), (1,))
EXACT = lax.Precision.HIGHEST


def split(v):
    high = v.astype(BF16)
    return high, (v - high.astype(F32)).astype(BF16)


def parts(v, count):
    out = []
    for _ in range(count):
        piece = v.astype(BF16)
        out.append(piece)
        v = v - piece.astype(F32)
    return jnp.concatenate(out, axis=0)


def unit():
    i0 = lax.broadcasted_iota(jnp.int32, (T, T), 0)
    i1 = lax.broadcasted_iota(jnp.int32, (T, T), 1)
    return jnp.where(i0 == i1, 1.0, 0.0).astype(BF16)


def spread_out(rows, width):
    count = rows.shape[0]
    row = lax.broadcasted_iota(jnp.int32, (count, count * width), 0)
    lane = lax.broadcasted_iota(jnp.int32, (count, count * width), 1)
    place = jnp.where(lane // width == row, 1.0, 0.0).astype(BF16)
    return dot(parts(rows, 2), jnp.concatenate([place, place], axis=0), ((0,), (0,)))


def head_rows(heads, width):
    row = lax.broadcasted_iota(jnp.int32, (8, heads * width), 0)
    lane = lax.broadcasted_iota(jnp.int32, (8, heads * width), 1)
    return jnp.where(lane // width == row, 1.0, 0.0).astype(BF16)


def steps_kernel(heads, dt_ref, alog_ref, tab_ref, decay_ref):
    blocks = dt_ref.shape[1] // T
    rows = blocks * heads
    raw = jnp.concatenate([dt_ref[:, k * T : (k + 1) * T] for k in range(blocks)], axis=0)
    step = jnp.maximum(raw, 0.0) + jnp.log1p(jnp.exp(-jnp.abs(raw)))
    head = lax.broadcasted_iota(jnp.int32, (rows, T), 0) % heads
    scale = jnp.full((rows, T), alog_ref[0], F32)
    for h in range(1, heads):
        scale = jnp.where(head == h, alog_ref[h], scale)
    rate = -jnp.exp(scale) * step
    i0 = lax.broadcasted_iota(jnp.int32, (T, T), 0)
    i1 = lax.broadcasted_iota(jnp.int32, (T, T), 1)
    cum = dot(rate, jnp.where(i0 <= i1, 1.0, 0.0).astype(F32), precision=EXACT)
    r0 = lax.broadcasted_iota(jnp.int32, (rows, rows), 0)
    r1 = lax.broadcasted_iota(jnp.int32, (rows, rows), 1)
    same = (r0 % heads) == (r1 % heads)
    total = jnp.broadcast_to(cum[:, T - 1 : T], (rows, T))
    before = dot(jnp.where(same & (r1 // heads < r0 // heads), 1.0, 0.0).astype(F32), total, precision=EXACT)
    after = dot(jnp.where(same & (r1 // heads > r0 // heads), 1.0, 0.0).astype(F32), total, precision=EXACT)
    cum_all = before + cum
    rest = total - cum
    to_end = after + rest
    columns = [
        cum,
        step,
        step * jnp.exp(to_end),
        jnp.exp(cum_all),
        cum_all,
        to_end,
        step * jnp.exp(rest),
        jnp.exp(cum),
        jnp.log(step) - cum,
        jnp.exp(total),
    ]
    for k in range(blocks):
        for j, v in enumerate(columns):
            tab_ref[k, j * heads : (j + 1) * heads, :] = v[k * heads : (k + 1) * heads]
    decay_ref[...] = jnp.concatenate([jnp.exp((before + total)[rows - heads :, :])] * (8 // heads), axis=0)


def ends_kernel(
    heads, width, x_ref, dy_ref, b_ref, pb_ref, c_ref, pc_ref, tab_ref, decay_ref,
    msg_ref, xh_ref, xl_ref, yh_ref, yl_ref, bt_ref, ct_ref, ends, skips,
):
    step, last = pl.program_id(0), pl.num_programs(0) - 1
    ring = msg_ref.shape[0]
    full = heads * width
    state = 2 * b_ref.shape[0]
    eye = unit()

    @pl.when(step == 0)
    def _():
        ends[...] = jnp.zeros_like(ends)
        skips[...] = jnp.zeros_like(skips)

    ks = range(tab_ref.shape[0])
    at = [slice(k * T, (k + 1) * T) for k in ks]
    weights = [spread_out(tab_ref[k, 2 * heads : 4 * heads, :], width) for k in ks]
    bts = [jnp.concatenate([b_ref[:, at[k]], pb_ref[:, at[k]]], axis=0) for k in ks]
    cts = [jnp.concatenate([c_ref[:, at[k]], pc_ref[:, at[k]]], axis=0) for k in ks]
    turned = [dot(eye, jnp.concatenate([bts[k], cts[k]], axis=0), NT).astype(BF16) for k in ks]
    xw = [split(x_ref[at[k], :].astype(F32) * weights[k][:, :full]) for k in ks]
    yw = [split(dy_ref[at[k], :].astype(F32) * weights[k][:, full:]) for k in ks]
    u = ends[0] + sum(
        dot(jnp.concatenate([bts[k], bts[k]], axis=1), jnp.concatenate(xw[k], axis=0)) for k in ks
    )
    v = ends[1] + sum(
        dot(jnp.concatenate([cts[k], cts[k]], axis=1), jnp.concatenate(yw[k], axis=0)) for k in ks
    )
    skip = skips[...]
    for k in ks:
        xh_ref[at[k], :], xl_ref[at[k], :] = xw[k]
        yh_ref[at[k], :], yl_ref[at[k], :] = yw[k]
        bt_ref[at[k], :] = turned[k][:, :state]
        ct_ref[at[k], :] = turned[k][:, state:]
        skip = skip + jnp.sum((x_ref[at[k], :].astype(F32) * dy_ref[at[k], :].astype(F32)).reshape(T // 8, 8, full), axis=0)
    ends[0] = u
    ends[1] = v
    skips[...] = skip

    @pl.when(step == last)
    def _():
        part = state // ring
        total = jnp.sum(skip, axis=0, keepdims=True)
        lane = lax.broadcasted_iota(jnp.int32, (1, T), 1)
        decay = [
            jnp.where(lane < width, decay_ref[2 * i : 2 * i + 1, :], decay_ref[2 * i + 1 : 2 * i + 2, :])
            for i in range(heads // 2)
        ]
        rows = decay + [total[:, i * T : (i + 1) * T] for i in range(heads // 2)]
        extra = jnp.concatenate(rows + [jnp.zeros((8 - len(rows), T), F32)], axis=0)
        for i in range(ring):
            msg_ref[i, 0:part, 0:full] = u[i * part : (i + 1) * part]
            msg_ref[i, part : 2 * part, 0:full] = v[i * part : (i + 1) * part]
            msg_ref[i, :, full : full + 128] = extra


def relay_kernel(heads, got_ref, _, msg_ref, skip_ref):
    ring, tile, width = msg_ref.shape
    first = lax.broadcasted_iota(jnp.int32, (tile, width), 0) < tile // 2

    def decay(j):
        return jnp.concatenate([got_ref[j, i : i + 1, width : width + 128] for i in range(width // 128)], axis=1)

    state = jnp.zeros((tile, width), F32)
    skip = jnp.zeros((tile, 128), F32)
    for j in range(ring):
        msg_ref[j] = state
        state = decay(j) * state + got_ref[j, :, 0:width]
        skip = skip + got_ref[j, :, width : width + 128]
    parts = width // 128
    per = heads // parts
    row = lax.broadcasted_iota(jnp.int32, (8, 128), 0)
    lane = lax.broadcasted_iota(jnp.int32, (8, 128), 1) // (128 // per)
    out = jnp.zeros((8, 128), F32)
    for i in range(parts):
        out = jnp.where(row == i * per + lane, skip[parts + i : parts + i + 1], out)
    skip_ref[...] = out
    state = jnp.zeros((tile, width), F32)
    for j in reversed(range(ring)):
        msg_ref[j] = jnp.where(first, msg_ref[j], state)
        state = decay(j) * state + got_ref[j, :, 0:width]


def inner_kernel(heads, width, x_ref, dy_ref, b_ref, pb_ref, c_ref, pc_ref, bt_ref, tab_ref, gx_ref, gb_ref, gc_ref, read_ref):
    i0 = lax.broadcasted_iota(jnp.int32, (T, T), 0)
    i1 = lax.broadcasted_iota(jnp.int32, (T, T), 1)
    seen = i1 >= i0
    row = lax.broadcasted_iota(jnp.int32, (6 * heads, heads * T), 0) % heads
    lane = lax.broadcasted_iota(jnp.int32, (6 * heads, heads * T), 1) // T
    mine = row == lane
    ones = jnp.ones((3 * heads, T), BF16)
    ks = range(tab_ref.shape[0])
    hs = range(heads)
    at = [slice(k * T, (k + 1) * T) for k in ks]
    lanes = [slice(h * width, (h + 1) * width) for h in hs]

    def spread(k):
        source = jnp.concatenate([parts(tab_ref[k, 8 * heads : 9 * heads, :], 3), ones], axis=0)
        reader = jnp.concatenate([ones, parts(tab_ref[k, 0:heads, :], 3)], axis=0)
        reader = jnp.where(mine, jnp.concatenate([reader] * heads, axis=1).astype(F32), 0.0).astype(BF16)
        return dot(source, reader, ((0,), (0,)))

    spreads = [spread(k) for k in ks]
    bts = [jnp.concatenate([b_ref[:, at[k]], pb_ref[:, at[k]]], axis=0) for k in ks]
    cts = [jnp.concatenate([c_ref[:, at[k]], pc_ref[:, at[k]]], axis=0) for k in ks]
    scores = [dot(bt_ref[at[k], :], cts[k]) for k in ks]
    grams = [[dot(x_ref[at[k], lanes[h]], dy_ref[at[k], lanes[h]], NT) for h in hs] for k in ks]
    mixes, weights = [], []
    for k in ks:
        mixed, reads, pairs = jnp.zeros((T, T), F32), [], []
        for h in hs:
            decay = jnp.exp(jnp.where(seen, spreads[k][:, h * T : (h + 1) * T], -jnp.inf))
            term = decay * grams[k][h]
            mixed = mixed + term
            reads.append(jnp.sum(term * scores[k], axis=0, keepdims=True))
            pairs.append(jnp.concatenate(split(decay * scores[k]), axis=1))
        read_ref[k] = jnp.concatenate(reads + [jnp.zeros((8 - heads, T), F32)], axis=0)
        mixes.append(split(mixed))
        weights.append(pairs)
    for k in ks:
        for h in hs:
            dy = dy_ref[at[k], lanes[h]]
            gx_ref[at[k], lanes[h]] = dot(weights[k][h], jnp.concatenate([dy, dy], axis=0))
    for k in ks:
        mh, ml = mixes[k]
        bt, ct = bts[k], cts[k]
        gc_ref[:, at[k]] = dot(jnp.concatenate([bt, bt], axis=1), jnp.concatenate([mh, ml], axis=0))
        gb_ref[:, at[k]] = dot(jnp.concatenate([ct, ct], axis=1), jnp.concatenate([mh, ml], axis=1), NT)


def states_kernel(
    heads, width, x_ref, dy_ref, b_ref, pb_ref, c_ref, pc_ref, bt_ref, ct_ref, xd_ref, xe_ref, yd_ref, ye_ref,
    tab_ref, read_ref, dskip_ref, alog_ref, gxi_ref, gbi_ref, gci_ref,
    gx_ref, gb_ref, gc_ref, rows_ref, slope_ref, loga_ref, states, xs, held, sums,
):
    turn, half = pl.program_id(0), pl.num_programs(0) // 2
    count = tab_ref.shape[0]
    full = heads * width
    last = count * half

    def joined(own, other, at):
        return jnp.concatenate([own[:, at], other[:, at]], axis=0)

    def across(k):
        lane = lax.broadcasted_iota(jnp.int32, (1, T), 1)
        row = tab_ref[k, 9 * heads : 10 * heads, :]
        return jnp.concatenate(
            [jnp.where(lane < width, row[2 * i : 2 * i + 1], row[2 * i + 1 : 2 * i + 2]) for i in range(heads // 2)], axis=1
        )

    @pl.when(turn == 0)
    def _():
        held[...] = jnp.zeros_like(held)
        sums[...] = jnp.zeros_like(sums)

    def at(k):
        return slice(k * T, (k + 1) * T)

    @pl.when(turn < half)
    def _():
        ks = range(count)
        weights = [spread_out(tab_ref[k, 4 * heads : 7 * heads, :], width) for k in ks]
        bts = [joined(b_ref, pb_ref, at(k)) for k in ks]
        cts = [joined(c_ref, pc_ref, at(k)) for k in ks]
        bts = [jnp.concatenate([v, v], axis=1) for v in bts]
        cts = [jnp.concatenate([v, v], axis=1) for v in cts]
        pairs = [
            jnp.concatenate(split(x_ref[at(k), :].astype(F32) * weights[k][:, 2 * full :]), axis=0) for k in ks
        ]
        for k in ks:
            xs[turn * count + k] = pairs[k]
        gains = [dot(bts[k], pairs[k]) for k in ks]
        state = held[0]
        for k in ks:
            states[turn * count + k] = state
            state = across(k) * state + gains[k]
        xd = [(xd_ref[at(k), :].astype(F32) + xe_ref[at(k), :].astype(F32)) * weights[k][:, full : 2 * full] for k in ks]
        yd = [(yd_ref[at(k), :].astype(F32) + ye_ref[at(k), :].astype(F32)) * weights[k][:, 0:full] for k in ks]
        xd = [jnp.concatenate(split(v), axis=0) for v in xd]
        yd = [jnp.concatenate(split(v), axis=0) for v in yd]
        slope_x = held[1] + sum(dot(bts[k], xd[k]) for k in ks)
        slope_y = held[2] + sum(dot(cts[k], yd[k]) for k in ks)
        held[0] = state
        held[1] = slope_x
        held[2] = slope_y

        @pl.when(turn == half - 1)
        def _():
            states[last] = state
            slope_ref[0] = slope_x
            slope_ref[1] = slope_y
            held[0] = jnp.zeros_like(state)

    @pl.when(turn >= half)
    def _():
        ks = range(count)
        select = head_rows(heads, width)
        select2 = jnp.concatenate([select, select], axis=1)
        i0 = lax.broadcasted_iota(jnp.int32, (T, T), 0)
        i1 = lax.broadcasted_iota(jnp.int32, (T, T), 1)
        suffix = jnp.where(i0 >= i1, 1.0, 0.0).astype(BF16)
        lane = lax.broadcasted_iota(jnp.int32, (1, 128), 1)
        skips = jnp.concatenate(
            [jnp.where(lane < width, dskip_ref[2 * i], dskip_ref[2 * i + 1]) for i in range(heads // 2)], axis=1
        )
        last_lane = lax.broadcasted_iota(jnp.int32, (heads, T), 1) == T - 1
        base = (2 * half - 1 - turn) * count
        weights = [spread_out(tab_ref[k, 6 * heads : 8 * heads, :], width) for k in ks]
        yw = [dy_ref[at(k), :].astype(F32) * weights[k][:, full:] for k in ks]
        ys = [split(v) for v in yw]
        cts = [joined(c_ref, pc_ref, at(k)) for k in ks]
        gains = [
            dot(jnp.concatenate([cts[k], cts[k]], axis=1), jnp.concatenate([ys[k][0], ys[k][1]], axis=0)) for k in ks
        ]
        starts = [split(states[base + k]) for k in ks]
        carried = [
            dot(jnp.concatenate([ct_ref[at(k), :]] * 2, axis=1), jnp.concatenate(starts[k], axis=0)) for k in ks
        ]
        adjoint = held[0]
        ends, edges = [None] * count, [None] * count
        for k in reversed(ks):
            ends[k] = split(adjoint)
            edges[k] = jnp.sum(adjoint * states[base + k + 1], axis=0, keepdims=True)
            adjoint = across(k) * adjoint + gains[k]
        held[0] = adjoint
        for k in ks:
            sh, sl = starts[k]
            yh, yl = ys[k]
            gc_ref[:, at(k)] = gci_ref[:, at(k)] + dot(
                jnp.concatenate([sh, sh, sl], axis=1), jnp.concatenate([yh, yl, yh], axis=1), NT
            )
        returned = [
            dot(jnp.concatenate([bt_ref[at(k), :]] * 2, axis=1), jnp.concatenate(ends[k], axis=0)) for k in ks
        ]
        for k in ks:
            ah, al = ends[k]
            pair = xs[base + k]
            xh, xl = pair[0:T], pair[T:]
            gb_ref[:, at(k)] = gbi_ref[:, at(k)] + dot(
                jnp.concatenate([ah, ah, al], axis=1), jnp.concatenate([xh, xl, xh], axis=1), NT
            )
        gxs = [gxi_ref[at(k), :] + weights[k][:, :full] * returned[k] for k in ks]
        for k in ks:
            gx_ref[at(k), :] = gxs[k] + skips * dy_ref[at(k), :].astype(F32)
        pairs = [
            jnp.concatenate(
                [
                    jnp.concatenate(split(yw[k] * carried[k]), axis=1),
                    jnp.concatenate(split(x_ref[at(k), :].astype(F32) * gxs[k]), axis=1),
                ],
                axis=0,
            )
            for k in ks
        ]
        found = [dot(select2, v, NT)[0:heads] for v in pairs]
        edges = jnp.concatenate(edges + [jnp.zeros((T - count, full), F32)], axis=0)
        edges = dot(select2, jnp.concatenate(split(edges), axis=1), NT)[0:heads]
        change = [
            found[k][:, 0:T]
            + read_ref[k, 0:heads, :]
            - found[k][:, T:]
            + jnp.where(last_lane, edges[:, k : k + 1], 0.0)
            for k in ks
        ]
        change = split(jnp.concatenate(change, axis=0))
        rate = dot(jnp.concatenate(change, axis=0), suffix)
        rate = rate[0 : count * heads] + rate[count * heads :]
        loga = sums[...]
        for k in ks:
            mine = rate[k * heads : (k + 1) * heads]
            rows_ref[k, 0:heads, :] = mine
            rows_ref[k, heads:, :] = found[k][:, T:]
            loga = loga + tab_ref[k, heads : 2 * heads, :] * mine
        sums[...] = loga

        @pl.when(turn == 2 * half - 1)
        def _():
            row = lax.broadcasted_iota(jnp.int32, (heads, T), 0)
            speed = jnp.full((heads, T), alog_ref[0], F32)
            for h in range(1, heads):
                speed = jnp.where(row == h, alog_ref[h], speed)
            loga_ref[...] = jnp.concatenate([-jnp.exp(speed) * loga, jnp.zeros((8 - heads, T), F32)], axis=0)


def edge_kernel(heads, width, got_ref, msg_ref, slope_ref, loga_ref, tab_ref, start_ref, end_ref, edge_ref, sums_ref):
    ring, tile, full = got_ref.shape
    part = tile // 2
    blocks = tab_ref.shape[0]
    start = jnp.concatenate([got_ref[i, 0:part, :] for i in range(ring)], axis=0)
    end = jnp.concatenate([got_ref[i, part:, :] for i in range(ring)], axis=0)
    local_end = jnp.concatenate([msg_ref[i, 0:part, 0:full] for i in range(ring)], axis=0)
    decay = jnp.concatenate([msg_ref[0, i : i + 1, full : full + 128] for i in range(full // 128)], axis=1)
    start_ref[0], start_ref[1] = split(start)
    end_ref[0], end_ref[1] = split(end)
    both = decay * jnp.sum(end * start, axis=0, keepdims=True)
    edge_ref[...] = jnp.broadcast_to(both + jnp.sum(end * local_end, axis=0, keepdims=True), (8, full))
    total = tab_ref[blocks - 1, 4 * heads : 5 * heads, T - 1 : T]
    row = lax.broadcasted_iota(jnp.int32, (heads, full), 0)
    lane = lax.broadcasted_iota(jnp.int32, (heads, full), 1)
    cross = jnp.sum(start * slope_ref[1] + end * slope_ref[0], axis=0, keepdims=True) + jnp.zeros((heads, full), F32)
    cross = jnp.where(lane // width == row, cross + total * both, 0.0)
    sums = loga_ref[0:heads, :]
    for i in range(full // T):
        sums = sums + cross[:, i * T : (i + 1) * T]
    sums = jnp.concatenate([sums, jnp.zeros((8 - heads, T), F32)], axis=0)
    for i in range(ring):
        sums_ref[i] = sums


def give_kernel(start_ref, end_ref, xh_ref, xl_ref, yh_ref, yl_ref, gbl_ref, gcl_ref, keep_ref, give_ref):
    sh, sl, eh, el = start_ref[0], start_ref[1], end_ref[0], end_ref[1]
    s3 = jnp.concatenate([sh, sh, sl], axis=1)
    e3 = jnp.concatenate([eh, eh, el], axis=1)
    half = keep_ref.shape[0] // 2
    wide = 2 * T
    for k in range(xh_ref.shape[0] // wide):
        at = slice(k * wide, (k + 1) * wide)
        xh, xl, yh, yl = xh_ref[at, :], xl_ref[at, :], yh_ref[at, :], yl_ref[at, :]
        gc = gcl_ref[:, at] + dot(s3, jnp.concatenate([yh, yl, yh], axis=1), NT)
        gb = gbl_ref[:, at] + dot(e3, jnp.concatenate([xh, xl, xh], axis=1), NT)
        keep_ref[0:half, at] = gb[0:half]
        keep_ref[half:, at] = gc[0:half]
        give_ref[0:half, at] = gb[half:]
        give_ref[half:, at] = gc[half:]


def finish_kernel(
    heads, width, start_ref, end_ref, edge_ref, xh_ref, xl_ref, yh_ref, yl_ref, b_ref, c_ref, tab_ref, rows_ref, dt_ref,
    alog_ref, gxl_ref, gx_ref, gdt_ref, diffs,
):
    turn, last = pl.program_id(0), pl.num_programs(0) - 1
    full = heads * width
    blocks = tab_ref.shape[0]
    count = xh_ref.shape[0] // T
    s2 = start_ref[...].reshape(2 * 128, full)
    e2 = end_ref[...].reshape(2 * 128, full)
    select = head_rows(heads, width)
    select2 = jnp.concatenate([select, select], axis=1)
    ks = range(count)
    at = [slice(k * T, (k + 1) * T) for k in ks]
    carried = [dot(jnp.concatenate([c_ref[at[k], :]] * 2, axis=1), s2) for k in ks]
    returned = [dot(jnp.concatenate([b_ref[at[k], :]] * 2, axis=1), e2) for k in ks]
    weights = [spread_out(tab_ref[turn * count + k, 2 * heads : 3 * heads, :], width) for k in ks]
    ya = [split((yh_ref[at[k], :].astype(F32) + yl_ref[at[k], :].astype(F32)) * carried[k]) for k in ks]
    xb = [split((xh_ref[at[k], :].astype(F32) + xl_ref[at[k], :].astype(F32)) * returned[k]) for k in ks]
    pairs = [jnp.concatenate([jnp.concatenate(ya[k], axis=1), jnp.concatenate(xb[k], axis=1)], axis=0) for k in ks]
    found = [dot(select2, v, NT)[0:heads] for v in pairs]
    for k in ks:
        gx_ref[at[k], :] = (gxl_ref[at[k], :] + weights[k] * returned[k]).astype(BF16)
        diffs[turn * count + k, 0:heads, :] = found[k][:, :T]
        diffs[turn * count + k, heads:, :] = found[k][:, T:]

    @pl.when(turn == last)
    def _():
        rows = blocks * heads
        edge = jnp.broadcast_to(edge_ref[0:1, :], (T, full))
        edge_rows = dot(select2, jnp.concatenate(split(edge), axis=1), NT)[0:heads]

        def gathered(ref, base):
            return jnp.concatenate([ref[k, base : base + heads, :] for k in range(blocks)], axis=0)

        own = gathered(diffs, heads)
        diff = gathered(diffs, 0) - own
        i0 = lax.broadcasted_iota(jnp.int32, (T, T), 0)
        i1 = lax.broadcasted_iota(jnp.int32, (T, T), 1)
        within = dot(diff, jnp.where(i0 >= i1, 1.0, 0.0).astype(F32), precision=EXACT)
        r0 = lax.broadcasted_iota(jnp.int32, (rows, rows), 0)
        r1 = lax.broadcasted_iota(jnp.int32, (rows, rows), 1)
        later = (r0 % heads == r1 % heads) & (r1 // heads > r0 // heads)
        after = dot(
            jnp.where(later, 1.0, 0.0).astype(F32), jnp.broadcast_to(within[:, 0:1], (rows, T)), precision=EXACT
        )
        rate_grad = gathered(rows_ref, 0) + within + after + jnp.concatenate([edge_rows] * blocks, axis=0)
        step = gathered(tab_ref, heads)
        head = lax.broadcasted_iota(jnp.int32, (rows, T), 0) % heads
        scale = jnp.full((rows, T), alog_ref[0], F32)
        for h in range(1, heads):
            scale = jnp.where(head == h, alog_ref[h], scale)
        raw = jnp.concatenate([dt_ref[:, k * T : (k + 1) * T] for k in range(blocks)], axis=0)
        slope = 1.0 / (1.0 + jnp.exp(-raw))
        gdt = ((gathered(rows_ref, heads) + own) / step - jnp.exp(scale) * rate_grad) * slope
        for k in range(blocks):
            gdt_ref[:, k * T : (k + 1) * T] = gdt[k * heads : (k + 1) * heads]


def join_kernel(keep_ref, back_ref, gb_ref, gc_ref):
    half = gb_ref.shape[0]
    gb_ref[...] = (keep_ref[0:half, :] + back_ref[0:half, :]).astype(BF16)
    gc_ref[...] = (keep_ref[half:, :] + back_ref[half:, :]).astype(BF16)


def call(kernel, name, turns, ins, outs, scratch=(), flops=10**6):
    def spec(how, shape):
        if how == "s":
            return pl.BlockSpec(memory_space=pltpu.SMEM)
        if how == "a":
            return pl.BlockSpec(memory_space=pl.ANY)
        if how == "w":
            return pl.BlockSpec(shape, lambda i: (0,) * len(shape))
        dim, cuts, place = how
        block = tuple(n // cuts if d == dim else n for d, n in enumerate(shape))
        return pl.BlockSpec(block, lambda i: tuple(place(i) if d == dim else 0 for d in range(len(shape))))

    def run(*args):
        return pl.pallas_call(
            kernel,
            name=name,
            grid=(turns,),
            out_shape=tuple(shape for shape, _ in outs),
            in_specs=[spec(how, a.shape) for how, a in zip(ins, args, strict=True)],
            out_specs=tuple(spec(how, shape.shape) for shape, how in outs),
            scratch_shapes=list(scratch),
            compiler_params=pltpu.CompilerParams(vmem_limit_bytes=VMEM_LIMIT),
            cost_estimate=pl.CostEstimate(flops=flops, bytes_accessed=flops // 10, transcendentals=0),
        )(*args)

    return run


def per_device(x, dt_raw, a_log, b_in, c_in, d_skip, dy):
    pairs = [(i, i ^ 1) for i in range(lax.axis_size("exp"))]
    ring = lax.axis_size("ctx")
    tokens, full = x.shape
    heads = dt_raw.shape[1]
    width = full // heads
    half = b_in.shape[1]
    state = 2 * half
    blocks = tokens // T
    n = TURNS
    shape = jax.ShapeDtypeStruct
    b, c, dt = b_in.T, c_in.T, dt_raw.T
    pb = lax.ppermute(b, "exp", pairs)
    pc = lax.ppermute(c, "exp", pairs)
    wide = shape((tokens, full), BF16)
    wide32 = shape((tokens, full), F32)
    long = shape((state, tokens), F32)
    narrow = shape((tokens, state), BF16)
    tile = shape((8, T), F32)
    pair = shape((2, state, full), BF16)
    part = functools.partial
    rows, cols = (0, n, lambda i: i), (1, n, lambda i: i)
    tab, decay = call(
        part(steps_kernel, heads), "steps", 1, "ws", [(shape((blocks, 10 * heads, T), F32), "w"), (tile, "w")]
    )(dt, a_log)
    msg, xh, xl, yh, yl, bt, ct = call(
        part(ends_kernel, heads, width),
        "ends",
        n,
        [rows, rows, cols, cols, cols, cols, rows, "w"],
        [(shape((ring, 8, full + 128), F32), "w")] + [(wide, rows)] * 4 + [(narrow, rows)] * 2,
        [pltpu.VMEM((2, state, full), F32), pltpu.VMEM((8, full), F32)],
    )(x, dy, b, pb, c, pc, tab, decay)
    got = lax.all_to_all(msg, "ctx", 0, 0, tiled=True)
    gxi, gbi, gci, read = call(
        part(inner_kernel, heads, width),
        "inner",
        n,
        [rows, rows, cols, cols, cols, cols, rows, rows],
        [(wide32, rows), (long, cols), (long, cols), (shape((blocks, 8, T), F32), rows)],
        flops=10**10,
    )(x, dy, b, pb, c, pc, bt, tab)
    sent, skip = call(
        part(relay_kernel, heads), "relay", 1, "wa", [(shape((ring, 8, full), F32), "w"), (tile, "w")]
    )(got, read)
    carry = lax.all_to_all(sent, "ctx", 0, 0, tiled=True)
    there_and_back = lambda i: jnp.where(i < n, i, 2 * n - 1 - i)
    forth = lambda i: jnp.minimum(i, n - 1)
    back_only = lambda i: jnp.where(i < n, n - 1, 2 * n - 1 - i)
    trows, tcols = (0, n, there_and_back), (1, n, there_and_back)
    frows = (0, n, forth)
    brows, bcols = (0, n, back_only), (1, n, back_only)
    gxl, gbl, gcl, rate, slopes, loga = call(
        part(states_kernel, heads, width),
        "states",
        2 * n,
        [trows, brows, tcols, tcols, tcols, tcols, brows, brows, frows, frows, frows, frows, trows, brows, "s", "s", brows]
        + [bcols, bcols],
        [(wide32, brows), (long, bcols), (long, bcols), (shape((blocks, 2 * heads, T), F32), brows)]
        + [(shape((2, state, full), F32), "w"), (tile, "w")],
        [
            pltpu.VMEM((blocks + 1, state, full), F32),
            pltpu.VMEM((blocks, 2 * T, full), BF16),
            pltpu.VMEM((3, state, full), F32),
            pltpu.VMEM((heads, T), F32),
        ],
        flops=10**10,
    )(x, dy, b, pb, c, pc, bt, ct, xh, xl, yh, yl, tab, read, d_skip, a_log, gxi, gbi, gci)
    start, end, edge, sums = call(
        part(edge_kernel, heads, width),
        "edge",
        1,
        "wwwww",
        [(pair, "w"), (pair, "w"), (shape((8, full), F32), "w"), (shape((ring, 8, T), F32), "w")],
    )(carry, msg, slopes, loga, tab)
    loga_all = lax.all_to_all(sums, "ctx", 0, 0, tiled=True)
    keep, give = call(
        give_kernel, "give", n, ["w", "w", rows, rows, rows, rows, cols, cols], [(long, cols)] * 2, flops=10**6
    )(start, end, xh, xl, yh, yl, gbl, gcl)
    back = lax.ppermute(give, "exp", pairs)
    gx, gdt = call(
        part(finish_kernel, heads, width),
        "finish",
        n,
        ["w", "w", "w"] + [rows] * 6 + ["w", "w", "w", "s", rows],
        [(wide, rows), (shape((heads, tokens), F32), "w")],
        [pltpu.VMEM((blocks, 2 * heads, T), F32)],
        flops=10**6,
    )(start, end, edge, xh, xl, yh, yl, bt, ct, tab, rate, dt, a_log, gxl)
    out = shape((half, tokens), BF16)
    gb, gc = call(join_kernel, "join", n, [cols, cols], [(out, cols)] * 2)(keep, back)
    grad_skip = jnp.sum(skip[0:heads], axis=1)
    grad_loga = jnp.sum(loga_all[:, 0:heads, :], axis=(0, 2))
    return gx, gdt.T, grad_loga, gb.T, gc.T, grad_skip


def solution(mesh):
    return jax.shard_map(
        per_device,
        mesh=mesh,
        in_specs=(P("ctx", "exp"), P("ctx", "exp"), P("exp"), P("ctx", "exp"), P("ctx", "exp"), P("exp"), P("ctx", "exp")),
        out_specs=(P("ctx", "exp"), P("ctx", "exp"), P("exp"), P("ctx", "exp"), P("ctx", "exp"), P("exp")),
        check_vma=False,
    )
```

```python
import functools

import jax
import jax.numpy as jnp
from jax import lax
from jax.experimental import pallas as pl
from jax.experimental.pallas import tpu as pltpu
from jax.sharding import PartitionSpec as P

T = 128
F32 = jnp.float32
BF16 = jnp.bfloat16
VMEM_LIMIT = 56 * 2**20
TURNS = 2


def dot(a, b, contract=((1,), (0,)), precision=None):
    return lax.dot_general(a, b, (contract, ((), ())), precision=precision, preferred_element_type=F32)


NT = ((1,), (1,))
EXACT = lax.Precision.HIGHEST


def split(v):
    high = v.astype(BF16)
    return high, (v - high.astype(F32)).astype(BF16)


def parts(v, count):
    out = []
    for _ in range(count):
        piece = v.astype(BF16)
        out.append(piece)
        v = v - piece.astype(F32)
    return jnp.concatenate(out, axis=0)


def unit():
    i0 = lax.broadcasted_iota(jnp.int32, (T, T), 0)
    i1 = lax.broadcasted_iota(jnp.int32, (T, T), 1)
    return jnp.where(i0 == i1, 1.0, 0.0).astype(BF16)


def spread_out(rows, width):
    count = rows.shape[0]
    row = lax.broadcasted_iota(jnp.int32, (count, count * width), 0)
    lane = lax.broadcasted_iota(jnp.int32, (count, count * width), 1)
    place = jnp.where(lane // width == row, 1.0, 0.0).astype(BF16)
    return dot(parts(rows, 2), jnp.concatenate([place, place], axis=0), ((0,), (0,)))


def head_rows(heads, width):
    row = lax.broadcasted_iota(jnp.int32, (8, heads * width), 0)
    lane = lax.broadcasted_iota(jnp.int32, (8, heads * width), 1)
    return jnp.where(lane // width == row, 1.0, 0.0).astype(BF16)


def steps_kernel(heads, dt_ref, alog_ref, tab_ref, decay_ref):
    blocks = dt_ref.shape[1] // T
    rows = blocks * heads
    raw = jnp.concatenate([dt_ref[:, k * T : (k + 1) * T] for k in range(blocks)], axis=0)
    step = jnp.maximum(raw, 0.0) + jnp.log1p(jnp.exp(-jnp.abs(raw)))
    head = lax.broadcasted_iota(jnp.int32, (rows, T), 0) % heads
    scale = jnp.full((rows, T), alog_ref[0], F32)
    for h in range(1, heads):
        scale = jnp.where(head == h, alog_ref[h], scale)
    rate = -jnp.exp(scale) * step
    i0 = lax.broadcasted_iota(jnp.int32, (T, T), 0)
    i1 = lax.broadcasted_iota(jnp.int32, (T, T), 1)
    cum = dot(rate, jnp.where(i0 <= i1, 1.0, 0.0).astype(F32), precision=EXACT)
    r0 = lax.broadcasted_iota(jnp.int32, (rows, rows), 0)
    r1 = lax.broadcasted_iota(jnp.int32, (rows, rows), 1)
    same = (r0 % heads) == (r1 % heads)
    total = jnp.broadcast_to(cum[:, T - 1 : T], (rows, T))
    before = dot(jnp.where(same & (r1 // heads < r0 // heads), 1.0, 0.0).astype(F32), total, precision=EXACT)
    after = dot(jnp.where(same & (r1 // heads > r0 // heads), 1.0, 0.0).astype(F32), total, precision=EXACT)
    cum_all = before + cum
    rest = total - cum
    to_end = after + rest
    columns = [
        cum,
        step,
        step * jnp.exp(to_end),
        jnp.exp(cum_all),
        cum_all,
        to_end,
        step * jnp.exp(rest),
        jnp.exp(cum),
        jnp.log(step) - cum,
        jnp.exp(total),
    ]
    for k in range(blocks):
        for j, v in enumerate(columns):
            tab_ref[k, j * heads : (j + 1) * heads, :] = v[k * heads : (k + 1) * heads]
    decay_ref[...] = jnp.concatenate([jnp.exp((before + total)[rows - heads :, :])] * (8 // heads), axis=0)


def ends_kernel(
    heads, width, x_ref, dy_ref, b_ref, pb_ref, c_ref, pc_ref, tab_ref, decay_ref,
    msg_ref, xh_ref, xl_ref, yh_ref, yl_ref, bt_ref, ct_ref, ends, skips,
):
    step, last = pl.program_id(0), pl.num_programs(0) - 1
    ring = msg_ref.shape[0]
    full = heads * width
    state = 2 * b_ref.shape[0]
    eye = unit()

    @pl.when(step == 0)
    def _():
        ends[...] = jnp.zeros_like(ends)
        skips[...] = jnp.zeros_like(skips)

    ks = range(tab_ref.shape[0])
    at = [slice(k * T, (k + 1) * T) for k in ks]
    weights = [spread_out(tab_ref[k, 2 * heads : 4 * heads, :], width) for k in ks]
    bts = [jnp.concatenate([b_ref[:, at[k]], pb_ref[:, at[k]]], axis=0) for k in ks]
    cts = [jnp.concatenate([c_ref[:, at[k]], pc_ref[:, at[k]]], axis=0) for k in ks]
    turned = [dot(eye, jnp.concatenate([bts[k], cts[k]], axis=0), NT).astype(BF16) for k in ks]
    xw = [split(x_ref[at[k], :].astype(F32) * weights[k][:, :full]) for k in ks]
    yw = [split(dy_ref[at[k], :].astype(F32) * weights[k][:, full:]) for k in ks]
    u = ends[0] + sum(
        dot(jnp.concatenate([bts[k], bts[k]], axis=1), jnp.concatenate(xw[k], axis=0)) for k in ks
    )
    v = ends[1] + sum(
        dot(jnp.concatenate([cts[k], cts[k]], axis=1), jnp.concatenate(yw[k], axis=0)) for k in ks
    )
    skip = skips[...]
    for k in ks:
        xh_ref[at[k], :], xl_ref[at[k], :] = xw[k]
        yh_ref[at[k], :], yl_ref[at[k], :] = yw[k]
        bt_ref[at[k], :] = turned[k][:, :state]
        ct_ref[at[k], :] = turned[k][:, state:]
        skip = skip + jnp.sum((x_ref[at[k], :].astype(F32) * dy_ref[at[k], :].astype(F32)).reshape(T // 8, 8, full), axis=0)
    ends[0] = u
    ends[1] = v
    skips[...] = skip

    @pl.when(step == last)
    def _():
        part = state // ring
        total = jnp.sum(skip, axis=0, keepdims=True)
        lane = lax.broadcasted_iota(jnp.int32, (1, T), 1)
        decay = [
            jnp.where(lane < width, decay_ref[2 * i : 2 * i + 1, :], decay_ref[2 * i + 1 : 2 * i + 2, :])
            for i in range(heads // 2)
        ]
        rows = decay + [total[:, i * T : (i + 1) * T] for i in range(heads // 2)]
        extra = jnp.concatenate(rows + [jnp.zeros((8 - len(rows), T), F32)], axis=0)
        for i in range(ring):
            msg_ref[i, 0:part, 0:full] = u[i * part : (i + 1) * part]
            msg_ref[i, part : 2 * part, 0:full] = v[i * part : (i + 1) * part]
            msg_ref[i, :, full : full + 128] = extra


def relay_kernel(heads, got_ref, _, msg_ref, skip_ref):
    ring, tile, width = msg_ref.shape
    first = lax.broadcasted_iota(jnp.int32, (tile, width), 0) < tile // 2

    def decay(j):
        return jnp.concatenate([got_ref[j, i : i + 1, width : width + 128] for i in range(width // 128)], axis=1)

    state = jnp.zeros((tile, width), F32)
    skip = jnp.zeros((tile, 128), F32)
    for j in range(ring):
        msg_ref[j] = state
        state = decay(j) * state + got_ref[j, :, 0:width]
        skip = skip + got_ref[j, :, width : width + 128]
    parts = width // 128
    per = heads // parts
    row = lax.broadcasted_iota(jnp.int32, (8, 128), 0)
    lane = lax.broadcasted_iota(jnp.int32, (8, 128), 1) // (128 // per)
    out = jnp.zeros((8, 128), F32)
    for i in range(parts):
        out = jnp.where(row == i * per + lane, skip[parts + i : parts + i + 1], out)
    skip_ref[...] = out
    state = jnp.zeros((tile, width), F32)
    for j in reversed(range(ring)):
        msg_ref[j] = jnp.where(first, msg_ref[j], state)
        state = decay(j) * state + got_ref[j, :, 0:width]


def inner_kernel(heads, width, x_ref, dy_ref, b_ref, pb_ref, c_ref, pc_ref, bt_ref, tab_ref, gx_ref, gb_ref, gc_ref, read_ref):
    i0 = lax.broadcasted_iota(jnp.int32, (T, T), 0)
    i1 = lax.broadcasted_iota(jnp.int32, (T, T), 1)
    seen = i1 >= i0
    row = lax.broadcasted_iota(jnp.int32, (6 * heads, heads * T), 0) % heads
    lane = lax.broadcasted_iota(jnp.int32, (6 * heads, heads * T), 1) // T
    mine = row == lane
    ones = jnp.ones((3 * heads, T), BF16)
    ks = range(tab_ref.shape[0])
    hs = range(heads)
    at = [slice(k * T, (k + 1) * T) for k in ks]
    lanes = [slice(h * width, (h + 1) * width) for h in hs]

    def spread(k):
        source = jnp.concatenate([parts(tab_ref[k, 8 * heads : 9 * heads, :], 3), ones], axis=0)
        reader = jnp.concatenate([ones, parts(tab_ref[k, 0:heads, :], 3)], axis=0)
        reader = jnp.where(mine, jnp.concatenate([reader] * heads, axis=1).astype(F32), 0.0).astype(BF16)
        return dot(source, reader, ((0,), (0,)))

    spreads = [spread(k) for k in ks]
    bts = [jnp.concatenate([b_ref[:, at[k]], pb_ref[:, at[k]]], axis=0) for k in ks]
    cts = [jnp.concatenate([c_ref[:, at[k]], pc_ref[:, at[k]]], axis=0) for k in ks]
    scores = [dot(bt_ref[at[k], :], cts[k]) for k in ks]
    grams = [[dot(x_ref[at[k], lanes[h]], dy_ref[at[k], lanes[h]], NT) for h in hs] for k in ks]
    mixes, weights = [], []
    for k in ks:
        mixed, reads, pairs = jnp.zeros((T, T), F32), [], []
        for h in hs:
            decay = jnp.exp(jnp.where(seen, spreads[k][:, h * T : (h + 1) * T], -jnp.inf))
            term = decay * grams[k][h]
            mixed = mixed + term
            reads.append(jnp.sum(term * scores[k], axis=0, keepdims=True))
            pairs.append(jnp.concatenate(split(decay * scores[k]), axis=1))
        read_ref[k] = jnp.concatenate(reads + [jnp.zeros((8 - heads, T), F32)], axis=0)
        mixes.append(split(mixed))
        weights.append(pairs)
    for k in ks:
        for h in hs:
            dy = dy_ref[at[k], lanes[h]]
            gx_ref[at[k], lanes[h]] = dot(weights[k][h], jnp.concatenate([dy, dy], axis=0))
    for k in ks:
        mh, ml = mixes[k]
        bt, ct = bts[k], cts[k]
        gc_ref[:, at[k]] = dot(jnp.concatenate([bt, bt], axis=1), jnp.concatenate([mh, ml], axis=0))
        gb_ref[:, at[k]] = dot(jnp.concatenate([ct, ct], axis=1), jnp.concatenate([mh, ml], axis=1), NT)


def states_kernel(
    heads, width, x_ref, dy_ref, b_ref, pb_ref, c_ref, pc_ref, bt_ref, ct_ref, xd_ref, xe_ref, yd_ref, ye_ref,
    tab_ref, read_ref, dskip_ref, alog_ref, gxi_ref, gbi_ref, gci_ref,
    gx_ref, gb_ref, gc_ref, rows_ref, slope_ref, loga_ref, states, xs, held, sums,
):
    turn, half = pl.program_id(0), pl.num_programs(0) // 2
    count = tab_ref.shape[0]
    full = heads * width
    last = count * half

    def joined(own, other, at):
        return jnp.concatenate([own[:, at], other[:, at]], axis=0)

    def across(k):
        lane = lax.broadcasted_iota(jnp.int32, (1, T), 1)
        row = tab_ref[k, 9 * heads : 10 * heads, :]
        return jnp.concatenate(
            [jnp.where(lane < width, row[2 * i : 2 * i + 1], row[2 * i + 1 : 2 * i + 2]) for i in range(heads // 2)], axis=1
        )

    @pl.when(turn == 0)
    def _():
        held[...] = jnp.zeros_like(held)
        sums[...] = jnp.zeros_like(sums)

    def at(k):
        return slice(k * T, (k + 1) * T)

    @pl.when(turn < half)
    def _():
        ks = range(count)
        weights = [spread_out(tab_ref[k, 4 * heads : 7 * heads, :], width) for k in ks]
        bts = [joined(b_ref, pb_ref, at(k)) for k in ks]
        cts = [joined(c_ref, pc_ref, at(k)) for k in ks]
        bts = [jnp.concatenate([v, v], axis=1) for v in bts]
        cts = [jnp.concatenate([v, v], axis=1) for v in cts]
        pairs = [
            jnp.concatenate(split(x_ref[at(k), :].astype(F32) * weights[k][:, 2 * full :]), axis=0) for k in ks
        ]
        for k in ks:
            xs[turn * count + k] = pairs[k]
        gains = [dot(bts[k], pairs[k]) for k in ks]
        state = held[0]
        for k in ks:
            states[turn * count + k] = state
            state = across(k) * state + gains[k]
        xd = [(xd_ref[at(k), :].astype(F32) + xe_ref[at(k), :].astype(F32)) * weights[k][:, full : 2 * full] for k in ks]
        yd = [(yd_ref[at(k), :].astype(F32) + ye_ref[at(k), :].astype(F32)) * weights[k][:, 0:full] for k in ks]
        xd = [jnp.concatenate(split(v), axis=0) for v in xd]
        yd = [jnp.concatenate(split(v), axis=0) for v in yd]
        slope_x = held[1] + sum(dot(bts[k], xd[k]) for k in ks)
        slope_y = held[2] + sum(dot(cts[k], yd[k]) for k in ks)
        held[0] = state
        held[1] = slope_x
        held[2] = slope_y

        @pl.when(turn == half - 1)
        def _():
            states[last] = state
            slope_ref[0] = slope_x
            slope_ref[1] = slope_y
            held[0] = jnp.zeros_like(state)

    @pl.when(turn >= half)
    def _():
        ks = range(count)
        select = head_rows(heads, width)
        select2 = jnp.concatenate([select, select], axis=1)
        i0 = lax.broadcasted_iota(jnp.int32, (T, T), 0)
        i1 = lax.broadcasted_iota(jnp.int32, (T, T), 1)
        suffix = jnp.where(i0 >= i1, 1.0, 0.0).astype(BF16)
        lane = lax.broadcasted_iota(jnp.int32, (1, 128), 1)
        skips = jnp.concatenate(
            [jnp.where(lane < width, dskip_ref[2 * i], dskip_ref[2 * i + 1]) for i in range(heads // 2)], axis=1
        )
        last_lane = lax.broadcasted_iota(jnp.int32, (heads, T), 1) == T - 1
        base = (2 * half - 1 - turn) * count
        weights = [spread_out(tab_ref[k, 6 * heads : 8 * heads, :], width) for k in ks]
        yw = [dy_ref[at(k), :].astype(F32) * weights[k][:, full:] for k in ks]
        ys = [split(v) for v in yw]
        cts = [joined(c_ref, pc_ref, at(k)) for k in ks]
        gains = [
            dot(jnp.concatenate([cts[k], cts[k]], axis=1), jnp.concatenate([ys[k][0], ys[k][1]], axis=0)) for k in ks
        ]
        starts = [split(states[base + k]) for k in ks]
        carried = [
            dot(jnp.concatenate([ct_ref[at(k), :]] * 2, axis=1), jnp.concatenate(starts[k], axis=0)) for k in ks
        ]
        adjoint = held[0]
        ends, edges = [None] * count, [None] * count
        for k in reversed(ks):
            ends[k] = split(adjoint)
            edges[k] = jnp.sum(adjoint * states[base + k + 1], axis=0, keepdims=True)
            adjoint = across(k) * adjoint + gains[k]
        held[0] = adjoint
        for k in ks:
            sh, sl = starts[k]
            yh, yl = ys[k]
            gc_ref[:, at(k)] = gci_ref[:, at(k)] + dot(
                jnp.concatenate([sh, sh, sl], axis=1), jnp.concatenate([yh, yl, yh], axis=1), NT
            )
        returned = [
            dot(jnp.concatenate([bt_ref[at(k), :]] * 2, axis=1), jnp.concatenate(ends[k], axis=0)) for k in ks
        ]
        for k in ks:
            ah, al = ends[k]
            pair = xs[base + k]
            xh, xl = pair[0:T], pair[T:]
            gb_ref[:, at(k)] = gbi_ref[:, at(k)] + dot(
                jnp.concatenate([ah, ah, al], axis=1), jnp.concatenate([xh, xl, xh], axis=1), NT
            )
        gxs = [gxi_ref[at(k), :] + weights[k][:, :full] * returned[k] for k in ks]
        for k in ks:
            gx_ref[at(k), :] = gxs[k] + skips * dy_ref[at(k), :].astype(F32)
        pairs = [
            jnp.concatenate(
                [
                    jnp.concatenate(split(yw[k] * carried[k]), axis=1),
                    jnp.concatenate(split(x_ref[at(k), :].astype(F32) * gxs[k]), axis=1),
                ],
                axis=0,
            )
            for k in ks
        ]
        found = [dot(select2, v, NT)[0:heads] for v in pairs]
        edges = jnp.concatenate(edges + [jnp.zeros((T - count, full), F32)], axis=0)
        edges = dot(select2, jnp.concatenate(split(edges), axis=1), NT)[0:heads]
        change = [
            found[k][:, 0:T]
            + read_ref[k, 0:heads, :]
            - found[k][:, T:]
            + jnp.where(last_lane, edges[:, k : k + 1], 0.0)
            for k in ks
        ]
        change = split(jnp.concatenate(change, axis=0))
        rate = dot(jnp.concatenate(change, axis=0), suffix)
        rate = rate[0 : count * heads] + rate[count * heads :]
        loga = sums[...]
        for k in ks:
            mine = rate[k * heads : (k + 1) * heads]
            rows_ref[k, 0:heads, :] = mine
            rows_ref[k, heads:, :] = found[k][:, T:]
            loga = loga + tab_ref[k, heads : 2 * heads, :] * mine
        sums[...] = loga

        @pl.when(turn == 2 * half - 1)
        def _():
            row = lax.broadcasted_iota(jnp.int32, (heads, T), 0)
            speed = jnp.full((heads, T), alog_ref[0], F32)
            for h in range(1, heads):
                speed = jnp.where(row == h, alog_ref[h], speed)
            loga_ref[...] = jnp.concatenate([-jnp.exp(speed) * loga, jnp.zeros((8 - heads, T), F32)], axis=0)


def edge_kernel(heads, width, got_ref, msg_ref, slope_ref, loga_ref, tab_ref, start_ref, end_ref, edge_ref, sums_ref):
    ring, tile, full = got_ref.shape
    part = tile // 2
    blocks = tab_ref.shape[0]
    start = jnp.concatenate([got_ref[i, 0:part, :] for i in range(ring)], axis=0)
    end = jnp.concatenate([got_ref[i, part:, :] for i in range(ring)], axis=0)
    local_end = jnp.concatenate([msg_ref[i, 0:part, 0:full] for i in range(ring)], axis=0)
    decay = jnp.concatenate([msg_ref[0, i : i + 1, full : full + 128] for i in range(full // 128)], axis=1)
    start_ref[0], start_ref[1] = split(start)
    end_ref[0], end_ref[1] = split(end)
    both = decay * jnp.sum(end * start, axis=0, keepdims=True)
    edge_ref[...] = jnp.broadcast_to(both + jnp.sum(end * local_end, axis=0, keepdims=True), (8, full))
    total = tab_ref[blocks - 1, 4 * heads : 5 * heads, T - 1 : T]
    row = lax.broadcasted_iota(jnp.int32, (heads, full), 0)
    lane = lax.broadcasted_iota(jnp.int32, (heads, full), 1)
    cross = jnp.sum(start * slope_ref[1] + end * slope_ref[0], axis=0, keepdims=True) + jnp.zeros((heads, full), F32)
    cross = jnp.where(lane // width == row, cross + total * both, 0.0)
    sums = loga_ref[0:heads, :]
    for i in range(full // T):
        sums = sums + cross[:, i * T : (i + 1) * T]
    sums = jnp.concatenate([sums, jnp.zeros((8 - heads, T), F32)], axis=0)
    for i in range(ring):
        sums_ref[i] = sums


def give_kernel(start_ref, end_ref, xh_ref, xl_ref, yh_ref, yl_ref, gbl_ref, gcl_ref, keep_ref, give_ref):
    sh, sl, eh, el = start_ref[0], start_ref[1], end_ref[0], end_ref[1]
    s3 = jnp.concatenate([sh, sh, sl], axis=1)
    e3 = jnp.concatenate([eh, eh, el], axis=1)
    half = keep_ref.shape[0] // 2
    wide = 2 * T
    for k in range(xh_ref.shape[0] // wide):
        at = slice(k * wide, (k + 1) * wide)
        xh, xl, yh, yl = xh_ref[at, :], xl_ref[at, :], yh_ref[at, :], yl_ref[at, :]
        gc = gcl_ref[:, at] + dot(s3, jnp.concatenate([yh, yl, yh], axis=1), NT)
        gb = gbl_ref[:, at] + dot(e3, jnp.concatenate([xh, xl, xh], axis=1), NT)
        keep_ref[0:half, at] = gb[0:half]
        keep_ref[half:, at] = gc[0:half]
        give_ref[0:half, at] = gb[half:]
        give_ref[half:, at] = gc[half:]


def finish_kernel(
    heads, width, start_ref, end_ref, edge_ref, xh_ref, xl_ref, yh_ref, yl_ref, b_ref, c_ref, tab_ref, rows_ref, dt_ref,
    alog_ref, gxl_ref, gbl_ref, gcl_ref, gx_ref, gdt_ref, keep_ref, give_ref, diffs,
):
    give_kernel(start_ref, end_ref, xh_ref, xl_ref, yh_ref, yl_ref, gbl_ref, gcl_ref, keep_ref, give_ref)
    turn, last = pl.program_id(0), pl.num_programs(0) - 1
    full = heads * width
    blocks = tab_ref.shape[0]
    count = xh_ref.shape[0] // T
    s2 = start_ref[...].reshape(2 * 128, full)
    e2 = end_ref[...].reshape(2 * 128, full)
    select = head_rows(heads, width)
    select2 = jnp.concatenate([select, select], axis=1)
    ks = range(count)
    at = [slice(k * T, (k + 1) * T) for k in ks]
    carried = [dot(jnp.concatenate([c_ref[at[k], :]] * 2, axis=1), s2) for k in ks]
    returned = [dot(jnp.concatenate([b_ref[at[k], :]] * 2, axis=1), e2) for k in ks]
    weights = [spread_out(tab_ref[turn * count + k, 2 * heads : 3 * heads, :], width) for k in ks]
    ya = [split((yh_ref[at[k], :].astype(F32) + yl_ref[at[k], :].astype(F32)) * carried[k]) for k in ks]
    xb = [split((xh_ref[at[k], :].astype(F32) + xl_ref[at[k], :].astype(F32)) * returned[k]) for k in ks]
    pairs = [jnp.concatenate([jnp.concatenate(ya[k], axis=1), jnp.concatenate(xb[k], axis=1)], axis=0) for k in ks]
    found = [dot(select2, v, NT)[0:heads] for v in pairs]
    for k in ks:
        gx_ref[at[k], :] = (gxl_ref[at[k], :] + weights[k] * returned[k]).astype(BF16)
        diffs[turn * count + k, 0:heads, :] = found[k][:, :T]
        diffs[turn * count + k, heads:, :] = found[k][:, T:]

    @pl.when(turn == last)
    def _():
        rows = blocks * heads
        edge = jnp.broadcast_to(edge_ref[0:1, :], (T, full))
        edge_rows = dot(select2, jnp.concatenate(split(edge), axis=1), NT)[0:heads]

        def gathered(ref, base):
            return jnp.concatenate([ref[k, base : base + heads, :] for k in range(blocks)], axis=0)

        own = gathered(diffs, heads)
        diff = gathered(diffs, 0) - own
        i0 = lax.broadcasted_iota(jnp.int32, (T, T), 0)
        i1 = lax.broadcasted_iota(jnp.int32, (T, T), 1)
        within = dot(diff, jnp.where(i0 >= i1, 1.0, 0.0).astype(F32), precision=EXACT)
        r0 = lax.broadcasted_iota(jnp.int32, (rows, rows), 0)
        r1 = lax.broadcasted_iota(jnp.int32, (rows, rows), 1)
        later = (r0 % heads == r1 % heads) & (r1 // heads > r0 // heads)
        after = dot(
            jnp.where(later, 1.0, 0.0).astype(F32), jnp.broadcast_to(within[:, 0:1], (rows, T)), precision=EXACT
        )
        rate_grad = gathered(rows_ref, 0) + within + after + jnp.concatenate([edge_rows] * blocks, axis=0)
        step = gathered(tab_ref, heads)
        head = lax.broadcasted_iota(jnp.int32, (rows, T), 0) % heads
        scale = jnp.full((rows, T), alog_ref[0], F32)
        for h in range(1, heads):
            scale = jnp.where(head == h, alog_ref[h], scale)
        raw = jnp.concatenate([dt_ref[:, k * T : (k + 1) * T] for k in range(blocks)], axis=0)
        slope = 1.0 / (1.0 + jnp.exp(-raw))
        gdt = ((gathered(rows_ref, heads) + own) / step - jnp.exp(scale) * rate_grad) * slope
        for k in range(blocks):
            gdt_ref[:, k * T : (k + 1) * T] = gdt[k * heads : (k + 1) * heads]


def join_kernel(keep_ref, back_ref, gb_ref, gc_ref):
    half = gb_ref.shape[0]
    gb_ref[...] = (keep_ref[0:half, :] + back_ref[0:half, :]).astype(BF16)
    gc_ref[...] = (keep_ref[half:, :] + back_ref[half:, :]).astype(BF16)


def call(kernel, name, turns, ins, outs, scratch=(), flops=10**6):
    def spec(how, shape):
        if how == "s":
            return pl.BlockSpec(memory_space=pltpu.SMEM)
        if how == "a":
            return pl.BlockSpec(memory_space=pl.ANY)
        if how == "w":
            return pl.BlockSpec(shape, lambda i: (0,) * len(shape))
        dim, cuts, place = how
        block = tuple(n // cuts if d == dim else n for d, n in enumerate(shape))
        return pl.BlockSpec(block, lambda i: tuple(place(i) if d == dim else 0 for d in range(len(shape))))

    def run(*args):
        return pl.pallas_call(
            kernel,
            name=name,
            grid=(turns,),
            out_shape=tuple(shape for shape, _ in outs),
            in_specs=[spec(how, a.shape) for how, a in zip(ins, args, strict=True)],
            out_specs=tuple(spec(how, shape.shape) for shape, how in outs),
            scratch_shapes=list(scratch),
            compiler_params=pltpu.CompilerParams(vmem_limit_bytes=VMEM_LIMIT),
            cost_estimate=pl.CostEstimate(flops=flops, bytes_accessed=flops // 10, transcendentals=0),
        )(*args)

    return run


def per_device(x, dt_raw, a_log, b_in, c_in, d_skip, dy):
    pairs = [(i, i ^ 1) for i in range(lax.axis_size("exp"))]
    ring = lax.axis_size("ctx")
    tokens, full = x.shape
    heads = dt_raw.shape[1]
    width = full // heads
    half = b_in.shape[1]
    state = 2 * half
    blocks = tokens // T
    n = TURNS
    shape = jax.ShapeDtypeStruct
    b, c, dt = b_in.T, c_in.T, dt_raw.T
    pb = lax.ppermute(b, "exp", pairs)
    pc = lax.ppermute(c, "exp", pairs)
    wide = shape((tokens, full), BF16)
    wide32 = shape((tokens, full), F32)
    long = shape((state, tokens), F32)
    narrow = shape((tokens, state), BF16)
    tile = shape((8, T), F32)
    pair = shape((2, state, full), BF16)
    part = functools.partial
    rows, cols = (0, n, lambda i: i), (1, n, lambda i: i)
    tab, decay = call(
        part(steps_kernel, heads), "steps", 1, "ws", [(shape((blocks, 10 * heads, T), F32), "w"), (tile, "w")]
    )(dt, a_log)
    msg, xh, xl, yh, yl, bt, ct = call(
        part(ends_kernel, heads, width),
        "ends",
        n,
        [rows, rows, cols, cols, cols, cols, rows, "w"],
        [(shape((ring, 8, full + 128), F32), "w")] + [(wide, rows)] * 4 + [(narrow, rows)] * 2,
        [pltpu.VMEM((2, state, full), F32), pltpu.VMEM((8, full), F32)],
    )(x, dy, b, pb, c, pc, tab, decay)
    got = lax.all_to_all(msg, "ctx", 0, 0, tiled=True)
    gxi, gbi, gci, read = call(
        part(inner_kernel, heads, width),
        "inner",
        n,
        [rows, rows, cols, cols, cols, cols, rows, rows],
        [(wide32, rows), (long, cols), (long, cols), (shape((blocks, 8, T), F32), rows)],
        flops=10**10,
    )(x, dy, b, pb, c, pc, bt, tab)
    sent, skip = call(
        part(relay_kernel, heads), "relay", 1, "wa", [(shape((ring, 8, full), F32), "w"), (tile, "w")]
    )(got, read)
    carry = lax.all_to_all(sent, "ctx", 0, 0, tiled=True)
    there_and_back = lambda i: jnp.where(i < n, i, 2 * n - 1 - i)
    forth = lambda i: jnp.minimum(i, n - 1)
    back_only = lambda i: jnp.where(i < n, n - 1, 2 * n - 1 - i)
    trows, tcols = (0, n, there_and_back), (1, n, there_and_back)
    frows = (0, n, forth)
    brows, bcols = (0, n, back_only), (1, n, back_only)
    gxl, gbl, gcl, rate, slopes, loga = call(
        part(states_kernel, heads, width),
        "states",
        2 * n,
        [trows, brows, tcols, tcols, tcols, tcols, brows, brows, frows, frows, frows, frows, trows, brows, "s", "s", brows]
        + [bcols, bcols],
        [(wide32, brows), (long, bcols), (long, bcols), (shape((blocks, 2 * heads, T), F32), brows)]
        + [(shape((2, state, full), F32), "w"), (tile, "w")],
        [
            pltpu.VMEM((blocks + 1, state, full), F32),
            pltpu.VMEM((blocks, 2 * T, full), BF16),
            pltpu.VMEM((3, state, full), F32),
            pltpu.VMEM((heads, T), F32),
        ],
        flops=10**10,
    )(x, dy, b, pb, c, pc, bt, ct, xh, xl, yh, yl, tab, read, d_skip, a_log, gxi, gbi, gci)
    start, end, edge, sums = call(
        part(edge_kernel, heads, width),
        "edge",
        1,
        "wwwww",
        [(pair, "w"), (pair, "w"), (shape((8, full), F32), "w"), (shape((ring, 8, T), F32), "w")],
    )(carry, msg, slopes, loga, tab)
    loga_all = lax.all_to_all(sums, "ctx", 0, 0, tiled=True)
    gx, gdt, keep, give = call(
        part(finish_kernel, heads, width),
        "finish",
        n,
        ["w", "w", "w"] + [rows] * 6 + ["w", "w", "w", "s", rows, cols, cols],
        [(wide, rows), (shape((heads, tokens), F32), "w"), (long, cols), (long, cols)],
        [pltpu.VMEM((blocks, 2 * heads, T), F32)],
        flops=10**10,
    )(start, end, edge, xh, xl, yh, yl, bt, ct, tab, rate, dt, a_log, gxl, gbl, gcl)
    give, loga_all = lax.optimization_barrier((give, loga_all))
    back = lax.ppermute(give, "exp", pairs)
    out = shape((half, tokens), BF16)
    gb, gc = call(join_kernel, "join", n, [cols, cols], [(out, cols)] * 2)(keep, back)
    grad_skip = jnp.sum(skip[0:heads], axis=1)
    grad_loga = jnp.sum(loga_all[:, 0:heads, :], axis=(0, 2))
    return gx, gdt.T, grad_loga, gb.T, gc.T, grad_skip


def solution(mesh):
    return jax.shard_map(
        per_device,
        mesh=mesh,
        in_specs=(P("ctx", "exp"), P("ctx", "exp"), P("exp"), P("ctx", "exp"), P("ctx", "exp"), P("exp"), P("ctx", "exp")),
        out_specs=(P("ctx", "exp"), P("ctx", "exp"), P("exp"), P("ctx", "exp"), P("ctx", "exp"), P("exp")),
        check_vma=False,
    )
```
